512 devices in a mesh: row: 16 (over y, x_hi, core), col: 32 (over z, x_lo).
Axes of the slice: x: 4 (x_hi: 2, x_lo: 2; x = x_hi * 2 + x_lo), y: 4, z: 16, core: 2. Of those that a mesh axis runs over, the one named last changes fastest.
Arguments:
- hess_inv: float32 [16384, 16384], P('row', 'col'), as said below
- weights: bfloat16 [6144, 16384], P('row', 'col'), may hold values from -6 to 6
- removed: int32 [512], replicated, may hold values from 0 to 16383, as said below
Outputs:
- hess_out: float32 [16384, 16384], P('row', 'col')
- weight_out: bfloat16 [6144, 16384], P('row', 'col')
The draws below stay inside these ranges and needn't reach their ends.
Inputs may be any that keep to these rules, and one draw needn't show every extreme that they name: `removed`: sorted ascending and distinct; each aligned block of 512 columns holds at most 48 of them, and at least one block holds exactly 48. `hess_inv`: symmetric and positive definite.
All inputs are finite; a program needn't handle non-finite values.
Results may differ from the reference program's by a relative error of at most 0.005.
Values may be sent and summed in bfloat16 or wider, within the bound.
A program may use at most 64 MiB of HBM per device.

```python
import math
import jax
import jax.numpy as jnp
from jax import lax

N = 16384
ROWS = 6144
TILE = 512
REMOVED = 512
MOST = 48


def draw_hess_inv(key, part):
    first_key, second_key, third_key, fourth_key = jax.random.split(jax.random.fold_in(key, 202), 4)
    factor_rank = 768
    noise_part = jax.random.normal(first_key, (N, N), jnp.float32)
    factor_part = jax.random.normal(third_key, (N, factor_rank), jnp.float32)
    diag_part = jax.random.uniform(second_key, (N,), jnp.float32, 1.5, 3.0)
    strength = 48.0
    log_reach = math.log(16.0)
    weight_mean = 46.0
    amplitude = jnp.exp(jax.random.uniform(fourth_key, (factor_rank,), jnp.float32, 0.0, log_reach))
    scaled_part = factor_part * amplitude[None, :]
    symmetric = (noise_part + noise_part.T) * (0.3536 / math.sqrt(N))
    shared = jnp.dot(scaled_part, scaled_part.T, precision=lax.Precision.HIGHEST) * (strength / (factor_rank * weight_mean))
    position = jnp.arange(N)
    return (symmetric + shared).at[position, position].add(diag_part)


def draw_removed(key, part):
    base_key = jax.random.fold_in(key, 101)
    first_key, second_key, third_key, fourth_key = jax.random.split(base_key, 4)
    tile_total = N // TILE
    full_tile = jax.random.randint(first_key, (), 0, tile_total)
    tile_caps = jax.random.randint(second_key, (tile_total,), MOST // 2, MOST + 1)
    tile_caps = jnp.where(jnp.arange(tile_total) == full_tile, 0, tile_caps)
    slot_tile = jnp.repeat(jnp.arange(tile_total), MOST)
    slot_rank = jnp.tile(jnp.arange(MOST), tile_total)
    usable = slot_rank < tile_caps[slot_tile]
    slot_score = jax.random.permutation(third_key, tile_total * MOST)
    slot_score = jnp.where(usable, slot_score, slot_score + tile_total * MOST)
    picked = jnp.argsort(slot_score)[:REMOVED - MOST]
    tile_keys = jax.random.split(fourth_key, tile_total)
    col_perms = jax.vmap(lambda inner: jax.random.permutation(inner, TILE))(tile_keys)
    full_cols = full_tile * TILE + col_perms[full_tile, :MOST]
    other_cols = slot_tile[picked] * TILE + col_perms[slot_tile[picked], slot_rank[picked]]
    return jnp.sort(jnp.concatenate([full_cols, other_cols])).astype(jnp.int32)


def block_levels(key, dims, cuts, least, largest):
    loudness = 1.0
    for dim, blocks in cuts:
        draws = jax.random.uniform(jax.random.fold_in(jax.random.fold_in(key, 6), dim), (blocks,), jnp.float32, least / len(cuts), largest / len(cuts))
        loudness = loudness * jnp.repeat(jnp.exp(draws), dims[dim] // blocks).reshape((-1,) + (1,) * (len(dims) - 1 - dim))
    return loudness


def noise(own_key, dims, spread, reach, shards=(), kind=jnp.bfloat16):
    drawn = jax.random.normal(own_key, dims, jnp.float32) * spread
    if len(shards) > 0:
        drawn = block_levels(own_key, dims, shards, -0.22, 0.18) * drawn
    return jnp.clip(drawn, min=-reach, max=reach).astype(kind)


def setup_inputs(seed: int = 0) -> dict:
    arg_keys = jax.random.split(jax.random.key(seed), 4)
    return {
        "hess_inv": draw_hess_inv(jax.random.fold_in(arg_keys[3], 71), 0),
        "weights": noise(arg_keys[1], (ROWS, N), 1.0, 6.0, ((0, 16), (1, 32))),
        "removed": draw_removed(jax.random.fold_in(arg_keys[3], 71), 0),
    }


def reference(hess_inv, weights, removed):
    block_rows = jnp.take(hess_inv, removed, axis=0)
    removed_block = jnp.take(block_rows, removed, axis=1)
    factor = jnp.linalg.cholesky(removed_block)
    identity = jnp.eye(removed_block.shape[0], dtype=jnp.float32)
    factor_inv = jax.scipy.linalg.solve_triangular(factor, identity, lower=True)
    block_inv = jnp.dot(factor_inv.T, factor_inv, precision=lax.Precision.HIGHEST)
    coupling = jnp.dot(block_inv, block_rows, precision=lax.Precision.HIGHEST)
    hess_cols = jnp.take(hess_inv, removed, axis=1)
    hess_out = hess_inv - jnp.dot(hess_cols, coupling, precision=lax.Precision.HIGHEST)
    weight_cols = jnp.take(weights, removed, axis=1).astype(jnp.float32)
    weight_out = (weights.astype(jnp.float32) - jnp.dot(weight_cols, coupling, precision=lax.Precision.HIGHEST)).astype(jnp.bfloat16)
    return (hess_out, weight_out)
```

```python
import functools

import jax
import jax.numpy as jnp
from jax import lax
from jax.experimental import pallas as pl
from jax.experimental.pallas import tpu as pltpu
from jax.sharding import PartitionSpec as P

MESH = pl.DeviceIdType.MESH
HIGHEST = lax.Precision.HIGHEST
LANES = 128


def all_bytes(ref, sem):
    return pltpu.make_async_copy(ref, ref, sem)


def exchange_kernel(
    rows,
    cols,
    hess_ref,
    weight_ref,
    rem_row_ref,
    rem_col_ref,
    block_ref,
    left_ref,
    upper_ref,
    wleft_ref,
    yt_ref,
    bp_ref,
    xh_ref,
    xw_ref,
    ra_ref,
    ru_ref,
    sb_ref,
    rb_ref,
    row_ref,
    rc_ref,
    rl_ref,
    rw_ref,
    send_sems,
    recv_sems,
    ring_send,
    ring_recv,
    wring_send,
    wring_recv,
):
    r = lax.axis_index("row")
    c = lax.axis_index("col")
    tall, wide = hess_ref.shape
    count = rem_col_ref.shape[0]
    groups = count // LANES
    share = count // rows
    zs = cols // 2
    wchunk = 16
    wowners = weight_ref.shape[0] // wchunk

    barrier = pltpu.get_barrier_semaphore()

    @pl.loop(1, rows)
    def _(k):
        pl.semaphore_signal(
            barrier, inc=1, device_id={"row": lax.rem(r + k, rows)}, device_id_type=MESH
        )

    @pl.loop(1, cols)
    def _(k):
        pl.semaphore_signal(
            barrier, inc=1, device_id={"col": lax.rem(c + k, cols)}, device_id_type=MESH
        )

    col_iota = lax.broadcasted_iota(jnp.int32, (wide, LANES), 0) + c * wide
    row_iota = lax.broadcasted_iota(jnp.int32, (LANES, tall), 1) + r * tall
    pick_col = jnp.zeros((wide, LANES), jnp.float32)
    pick_row = jnp.zeros((LANES, tall), jnp.float32)
    for g in range(groups):
        pick_col = jnp.where(rem_row_ref[g : g + 1, :] == col_iota, 1.0, pick_col)
        pick_row = jnp.where(
            rem_col_ref[g * LANES : (g + 1) * LANES, :] == row_iota, 1.0, pick_row
        )

    own_rows = jnp.dot(
        pick_row, hess_ref[...], precision=HIGHEST, preferred_element_type=jnp.float32
    )
    bp_ref[...] = jnp.dot(
        own_rows, pick_col, precision=HIGHEST, preferred_element_type=jnp.float32
    )
    pl.semaphore_wait(barrier, rows + cols - 2)

    def spread_rows(src, dst, which):
        @pl.loop(1, rows)
        def _(k):
            to = lax.rem(r + k, rows)
            pltpu.make_async_remote_copy(
                src_ref=src(to),
                dst_ref=dst,
                send_sem=send_sems.at[which],
                recv_sem=recv_sems.at[which],
                device_id={"row": to},
                device_id_type=MESH,
            ).start()

    def spread_cols(src, dst, which, limit):
        @pl.loop(1, cols)
        def _(k):
            to = lax.rem(c + k, cols)

            @pl.when(to < limit)
            def _():
                pltpu.make_async_remote_copy(
                    src_ref=src(to),
                    dst_ref=dst,
                    send_sem=send_sems.at[which],
                    recv_sem=recv_sems.at[which],
                    device_id={"col": to},
                    device_id_type=MESH,
                ).start()

    spread_rows(lambda to: bp_ref.at[pl.ds(lax.rem(to, 4) * share, share)], ra_ref.at[r], 0)
    ra_ref[r] = bp_ref[pl.ds(lax.rem(r, 4) * share, share), :]
    yt_ref[...] = own_rows.T
    spread_rows(lambda to: yt_ref.at[pl.ds(to * share, share)], ru_ref.at[r], 1)
    ru_ref[r] = yt_ref[pl.ds(r * share, share), :]

    xh_ref[...] = jnp.dot(
        hess_ref[...], pick_col, precision=HIGHEST, preferred_element_type=jnp.float32
    )
    xw_ref[...] = jnp.dot(
        weight_ref[...], pick_col.astype(jnp.bfloat16), preferred_element_type=jnp.float32
    ).astype(jnp.bfloat16)

    tile_row = [lax.shift_right_logical(rem_row_ref[g : g + 1, :], 9) for g in range(groups)]

    all_bytes(ra_ref.at[pl.ds(0, rows - 1)], recv_sems.at[0]).wait()
    own_src = lax.shift_right_logical(rem_col_ref[pl.ds(r * share, share), :], 10)
    strip = jnp.zeros((share, LANES), jnp.float32)
    for k in range(rows):
        strip = jnp.where(own_src == k, ra_ref[k], strip)
    for j in range(share):
        sb_ref[j] = strip[j : j + 1, :]
    spread_cols(lambda to: sb_ref.at[to], rb_ref.at[c], 2, cols)
    rb_ref[c] = sb_ref[c]

    all_bytes(ru_ref.at[pl.ds(0, rows - 1)], recv_sems.at[1]).wait()
    for g in range(groups):
        part = jnp.zeros((share, LANES), jnp.float32)
        src = lax.shift_right_logical(tile_row[g], 1)
        for k in range(rows):
            part = jnp.where(src == k, ru_ref[k], part)
        upper_ref[pl.ds(r * share, share), g * LANES : (g + 1) * LANES] = part

    all_bytes(rb_ref.at[pl.ds(0, cols - 1)], recv_sems.at[2]).wait()
    for g in range(groups):
        part = jnp.zeros((1, LANES), jnp.float32)
        for k in range(cols):
            part = jnp.where(tile_row[g] == k, rb_ref[k], part)
        row_ref[:, g * LANES : (g + 1) * LANES] = part
    spread_cols(lambda to: row_ref, rc_ref.at[c], 3, cols)
    rc_ref[c] = row_ref[...]

    spread_cols(lambda to: xh_ref.at[pl.ds(to * share, share)], rl_ref.at[c], 4, cols)
    rl_ref[c] = xh_ref[pl.ds(c * share, share), :]
    spread_cols(lambda to: xw_ref.at[pl.ds(to * wchunk, wchunk)], rw_ref.at[c], 5, wowners)

    all_bytes(rc_ref.at[pl.ds(0, cols - 1)], recv_sems.at[3]).wait()
    for j in range(share):
        block_ref[pl.ds(r * share + j, 1), :] = rc_ref[j]
    own_share = pl.ds(r * share, share)
    spread_rows(lambda to: block_ref.at[own_share], block_ref.at[own_share], 6)
    spread_rows(lambda to: upper_ref.at[own_share], upper_ref.at[own_share], 7)

    all_bytes(rl_ref.at[pl.ds(0, cols - 1)], recv_sems.at[4]).wait()
    own_left = pl.ds(c * share, share)
    for g in range(groups):

        def gather_left(k, part):
            return jnp.where(tile_row[g] == k, rl_ref[k], part)

        left_ref[own_left, g * LANES : (g + 1) * LANES] = lax.fori_loop(
            0, cols, gather_left, jnp.zeros((share, LANES), jnp.float32)
        )

    @pl.when(c < wowners)
    def _():
        rw_ref[c] = xw_ref[pl.ds(pl.multiple_of(c * wchunk, wchunk), wchunk), :]
        all_bytes(rw_ref.at[pl.ds(0, cols - 1)], recv_sems.at[5]).wait()
        for g in range(groups):

            def gather_weight(k, part):
                return jnp.where(tile_row[g] == k, rw_ref[k].astype(jnp.float32), part)

            wleft_ref[
                pl.ds(pl.multiple_of(c * wchunk, wchunk), wchunk), g * LANES : (g + 1) * LANES
            ] = lax.fori_loop(0, cols, gather_weight, jnp.zeros((wchunk, LANES), jnp.float32)).astype(
                jnp.bfloat16
            )

    sibling = c + 1 - 2 * lax.rem(c, 2)
    z = c // 2

    def left_copy(slot, size, step, to):
        where = pl.ds(slot * size, size)
        return pltpu.make_async_remote_copy(
            src_ref=left_ref.at[where],
            dst_ref=left_ref.at[where],
            send_sem=ring_send.at[step],
            recv_sem=ring_recv.at[step],
            device_id={"col": to},
            device_id_type=MESH,
        )

    def weight_copy(slot, size, step, to):
        where = pl.ds(pl.multiple_of(slot * size, size), size)
        return pltpu.make_async_remote_copy(
            src_ref=wleft_ref.at[where],
            dst_ref=wleft_ref.at[where],
            send_sem=wring_send.at[step],
            recv_sem=wring_recv.at[step],
            device_id={"col": to},
            device_id_type=MESH,
        )

    wz = wowners // 2
    last = zs - 1
    left_copy(c, share, last, sibling).start()

    @pl.when(z < wz)
    def _():
        weight_copy(c, wchunk, last, sibling).start()

    left_copy(sibling, share, last, sibling).wait_recv()

    @pl.when(z < wz)
    def _():
        weight_copy(sibling, wchunk, last, sibling).wait_recv()

    ways = []
    for s in range(zs // 2):
        ways.append((s, 1, s))
        if s < zs - 1 - zs // 2:
            ways.append((zs // 2 + s, -1, s))

    def z_of(step):
        return lax.rem(z + step + zs, zs)

    for step, way, s in ways:
        to = 2 * z_of(way) + lax.rem(c, 2)
        src = z_of(-way * s)
        if s > 0:
            left_copy(src, 2 * share, step - 1, to).wait_recv()
        left_copy(src, 2 * share, step, to).start()

        @pl.when(src < wz)
        def _():
            if s > 0:
                weight_copy(src, 2 * wchunk, step - 1, to).wait_recv()
            weight_copy(src, 2 * wchunk, step, to).start()

    ends = [(zs // 2 - 1, 1, zs // 2 - 1), (zs - 2, -1, zs - 2 - zs // 2)]
    for step, way, s in ends:
        src = z_of(-way * (s + 1))
        left_copy(src, 2 * share, step, sibling).wait_recv()

        @pl.when(src < wz)
        def _():
            weight_copy(src, 2 * wchunk, step, sibling).wait_recv()

    all_rows = pl.ds(0, (rows - 1) * share)
    all_bytes(block_ref.at[all_rows], recv_sems.at[6]).wait()
    all_bytes(upper_ref.at[all_rows], recv_sems.at[7]).wait()

    all_bytes(ra_ref.at[pl.ds(0, rows - 1)], send_sems.at[0]).wait()
    all_bytes(ru_ref.at[pl.ds(0, rows - 1)], send_sems.at[1]).wait()
    all_bytes(rb_ref.at[pl.ds(0, cols - 1)], send_sems.at[2]).wait()
    all_bytes(rc_ref.at[pl.ds(0, cols - 1)], send_sems.at[3]).wait()
    all_bytes(rl_ref.at[pl.ds(0, cols - 1)], send_sems.at[4]).wait()

    @pl.when(c < wowners)
    def _():
        all_bytes(rw_ref.at[pl.ds(0, wowners - 1)], send_sems.at[5]).wait()

    @pl.when(c >= wowners)
    def _():
        all_bytes(rw_ref.at[pl.ds(0, wowners)], send_sems.at[5]).wait()

    all_bytes(block_ref.at[all_rows], send_sems.at[6]).wait()
    all_bytes(upper_ref.at[all_rows], send_sems.at[7]).wait()
    left_copy(c, share, last, sibling).wait_send()

    @pl.when(z < wz)
    def _():
        weight_copy(c, wchunk, last, sibling).wait_send()

    for step, way, s in ways:
        src = z_of(-way * s)
        left_copy(src, 2 * share, step, sibling).wait_send()

        @pl.when(src < wz)
        def _():
            weight_copy(src, 2 * wchunk, step, sibling).wait_send()


def exchange(hess_inv, weights, removed):
    rows, cols = lax.axis_size("row"), lax.axis_size("col")
    tall, wide = hess_inv.shape
    count = removed.shape[0]
    share = count // rows
    zs = cols // 2
    vmem = pl.BlockSpec(memory_space=pltpu.VMEM)
    f32, bf16 = jnp.float32, jnp.bfloat16
    dma = pltpu.SemaphoreType.DMA
    return pl.pallas_call(
        functools.partial(exchange_kernel, rows, cols),
        out_shape=(
            jax.ShapeDtypeStruct((count, count), f32),
            jax.ShapeDtypeStruct((tall, count), f32),
            jax.ShapeDtypeStruct((wide, count), f32),
            jax.ShapeDtypeStruct((weights.shape[0], count), bf16),
        ),
        in_specs=[vmem] * 4,
        out_specs=(vmem,) * 4,
        scratch_shapes=[
            pltpu.VMEM((wide, LANES), f32),
            pltpu.VMEM((LANES, LANES), f32),
            pltpu.VMEM((tall, LANES), f32),
            pltpu.VMEM((weights.shape[0], LANES), bf16),
            pltpu.VMEM((rows, share, LANES), f32),
            pltpu.VMEM((rows, share, LANES), f32),
            pltpu.VMEM((share, 1, LANES), f32),
            pltpu.VMEM((cols, 1, LANES), f32),
            pltpu.VMEM((1, count), f32),
            pltpu.VMEM((cols, 1, count), f32),
            pltpu.VMEM((cols, share, LANES), f32),
            pltpu.VMEM((cols, 16, LANES), bf16),
            dma((8,)),
            dma((8,)),
            dma((zs,)),
            dma((zs,)),
            dma((zs,)),
            dma((zs,)),
        ],
        compiler_params=pltpu.CompilerParams(
            collective_id=0, has_side_effects=True, vmem_limit_bytes=48 * 1024 * 1024
        ),
        cost_estimate=pl.CostEstimate(
            flops=2 * tall * wide * LANES * 6, bytes_accessed=8 * 1024 * 1024, transcendentals=0
        ),
        name="exchange",
    )(hess_inv, weights, removed.reshape(count // LANES, LANES), removed.reshape(count, 1))


def on_device(hess_inv, weights, removed):
    block, left, upper, weight_left = exchange(hess_inv, weights, removed)
    factor = jnp.linalg.cholesky(block)
    identity = jnp.eye(block.shape[0], dtype=jnp.float32)
    factor_inv = jax.scipy.linalg.solve_triangular(factor, identity, lower=True)
    block_inv = jnp.dot(factor_inv.T, factor_inv, precision=HIGHEST)
    coupling = jnp.dot(block_inv, upper.T, precision=HIGHEST)
    hess_out = hess_inv - jnp.dot(left, coupling, precision=HIGHEST)
    weight_fix = jnp.dot(weight_left.astype(jnp.float32), coupling, precision=HIGHEST)
    weight_out = (weights.astype(jnp.float32) - weight_fix).astype(jnp.bfloat16)
    return (hess_out, weight_out)


def solution(mesh):
    placed = (P("row", "col"), P("row", "col"), P())
    return jax.shard_map(
        on_device,
        mesh=mesh,
        in_specs=placed,
        out_specs=(P("row", "col"), P("row", "col")),
        check_vma=False,
    )
```

```python
import functools

import jax
import jax.numpy as jnp
from jax import lax
from jax.experimental import pallas as pl
from jax.experimental.pallas import tpu as pltpu
from jax.sharding import PartitionSpec as P

MESH = pl.DeviceIdType.MESH
HIGHEST = lax.Precision.HIGHEST
LANES = 128


def all_bytes(ref, sem):
    return pltpu.make_async_copy(ref, ref, sem)


def split3(x):
    high = x.astype(jnp.bfloat16)
    rest = x - high.astype(jnp.float32)
    mid = rest.astype(jnp.bfloat16)
    return high, mid, (rest - mid.astype(jnp.float32)).astype(jnp.bfloat16)


def dot6(a, b, b_dim=0):
    ah, am, al = split3(a)
    bh, bm, bl = split3(b)
    return lax.dot_general(
        jnp.concatenate([ah, al, am, am, ah, ah], axis=1),
        jnp.concatenate([bl, bh, bm, bh, bm, bh], axis=b_dim),
        (((1,), (b_dim,)), ((), ())),
        preferred_element_type=jnp.float32,
    )


def eliminate(columns, panel):
    count = len(columns)
    sub = lax.broadcasted_iota(jnp.int32, (8, LANES), 0)

    def row(x, j):
        return jnp.broadcast_to(x[j // 8][j % 8 : j % 8 + 1, :], (8, LANES))

    todo = [list(x) for x in columns] + [list(panel)]
    for j in range(count):
        pivot = todo.pop(0)
        scale = 1.0 / row(pivot, j)
        for x in todo:
            new = row(x, j) * scale
            for t in range(len(x)):
                x[t] = x[t] - pivot[t] * new
            x[j // 8] = jnp.where(sub == j % 8, new, x[j // 8])
    return todo[0]


def invert_tile(tile):
    count = tile.shape[0] // 8
    v = [tile[8 * i : 8 * i + 8, :] for i in range(count)]
    lane = lax.broadcasted_iota(jnp.int32, (8, LANES), 1)
    sub = lax.broadcasted_iota(jnp.int32, (8, LANES), 0)

    def column(x, k):
        return jnp.broadcast_to(x[:, k : k + 1], (8, LANES))

    for b in range(count // 2):
        k = 16 * b
        rows = [2 * b, 2 * b + 1]
        ahead = [i for i in (2 * b + 2, 2 * b + 3) if i < count]
        rest = [i for i in range(count) if i not in rows and i not in ahead]
        inside = (lane >= k) & (lane < k + 16)
        columns = [[column(v[i], k + q) for i in rows] for q in range(16)]
        panel = [jnp.where(inside, jnp.where(lane == sub + 8 * i, 1.0, 0.0), v[i]) for i in rows]
        new = eliminate(columns, panel)
        w = list(v)
        for i in ahead:
            terms = [
                column(v[i], k + q)
                * jnp.broadcast_to(new[q // 8][q % 8 : q % 8 + 1, :], (8, LANES))
                for q in range(16)
            ]
            while len(terms) > 1:
                terms = [terms[z] + terms[z + 1] for z in range(0, len(terms), 2)]
            w[i] = jnp.where(inside, 0.0, v[i]) - terms[0]
        for t, i in enumerate(rows):
            w[i] = new[t]
        change = jnp.dot(
            jnp.concatenate([v[i] for i in rest], axis=0)[:, k : k + 16],
            jnp.concatenate(new, axis=0),
            precision=HIGHEST,
            preferred_element_type=jnp.float32,
        )
        for z, i in enumerate(rest):
            w[i] = jnp.where(inside, 0.0, v[i]) - change[8 * z : 8 * z + 8]
        v = w
    return jnp.concatenate(v, axis=0)


def exchange_kernel(
    rows,
    cols,
    hess_ref,
    weight_ref,
    rem_row_ref,
    rem_col_ref,
    coupling_ref,
    left_ref,
    wleft_ref,
    block_ref,
    upper_ref,
    strip_ref,
    yt_ref,
    bp_ref,
    xh_ref,
    xw_ref,
    ra_ref,
    ru_ref,
    sb_ref,
    rb_ref,
    row_ref,
    rc_ref,
    rl_ref,
    rw_ref,
    send_sems,
    recv_sems,
    ring_send,
    ring_recv,
    wring_send,
    wring_recv,
):
    r = lax.axis_index("row")
    c = lax.axis_index("col")
    tall, wide = hess_ref.shape
    count = rem_col_ref.shape[0]
    groups = count // LANES
    share = count // rows
    zs = cols // 2
    wchunk = 16
    wowners = weight_ref.shape[0] // wchunk

    barrier = pltpu.get_barrier_semaphore()

    @pl.loop(1, rows)
    def _(k):
        pl.semaphore_signal(
            barrier, inc=1, device_id={"row": lax.rem(r + k, rows)}, device_id_type=MESH
        )

    @pl.loop(1, cols)
    def _(k):
        pl.semaphore_signal(
            barrier, inc=1, device_id={"col": lax.rem(c + k, cols)}, device_id_type=MESH
        )

    col_iota = lax.broadcasted_iota(jnp.int32, (wide, LANES), 0) + c * wide
    row_iota = lax.broadcasted_iota(jnp.int32, (LANES, tall), 1) + r * tall
    pick_col = jnp.zeros((wide, LANES), jnp.float32)
    pick_row = jnp.zeros((LANES, tall), jnp.float32)
    for g in range(groups):
        pick_col = jnp.where(rem_row_ref[g : g + 1, :] == col_iota, 1.0, pick_col)
        pick_row = jnp.where(
            rem_col_ref[g * LANES : (g + 1) * LANES, :] == row_iota, 1.0, pick_row
        )

    own_rows = jnp.dot(
        pick_row, hess_ref[...], precision=HIGHEST, preferred_element_type=jnp.float32
    )
    bp_ref[...] = jnp.dot(
        own_rows, pick_col, precision=HIGHEST, preferred_element_type=jnp.float32
    )
    pl.semaphore_wait(barrier, rows + cols - 2)

    def spread_rows(src, dst, which):
        @pl.loop(1, rows)
        def _(k):
            to = lax.rem(r + k, rows)
            pltpu.make_async_remote_copy(
                src_ref=src(to),
                dst_ref=dst,
                send_sem=send_sems.at[which],
                recv_sem=recv_sems.at[which],
                device_id={"row": to},
                device_id_type=MESH,
            ).start()

    def spread_cols(src, dst, which, limit):
        @pl.loop(1, cols)
        def _(k):
            to = lax.rem(c + k, cols)

            @pl.when(to < limit)
            def _():
                pltpu.make_async_remote_copy(
                    src_ref=src(to),
                    dst_ref=dst,
                    send_sem=send_sems.at[which],
                    recv_sem=recv_sems.at[which],
                    device_id={"col": to},
                    device_id_type=MESH,
                ).start()

    spread_rows(lambda to: bp_ref.at[pl.ds(lax.rem(to, 4) * share, share)], ra_ref.at[r], 0)
    ra_ref[r] = bp_ref[pl.ds(lax.rem(r, 4) * share, share), :]
    yt_ref[...] = own_rows.T
    spread_rows(lambda to: yt_ref.at[pl.ds(to * share, share)], ru_ref.at[r], 1)
    ru_ref[r] = yt_ref[pl.ds(r * share, share), :]

    half = LANES // 2
    low = lax.broadcasted_iota(jnp.int32, (wide, LANES), 1) < half
    fold = pick_col + pltpu.roll(pick_col, half, 1)
    pick_half = jnp.concatenate(
        [jnp.where(low, fold, 0.0), jnp.where(low, 0.0, fold)], axis=0
    ).astype(jnp.bfloat16)
    parts = hess_ref[...].reshape(tall // share, 2, share // 2, wide)
    pairs = jnp.concatenate(
        [parts[:, 0].reshape(tall // 2, wide), parts[:, 1].reshape(tall // 2, wide)], axis=1
    )
    packed = [
        jnp.dot(x, pick_half, preferred_element_type=jnp.float32) for x in split3(pairs)
    ]
    xh_ref[...] = (packed[2] + packed[1]) + packed[0]
    xw_ref[...] = jnp.dot(
        weight_ref[...], pick_col.astype(jnp.bfloat16), preferred_element_type=jnp.float32
    ).astype(jnp.bfloat16)

    tile_row = [lax.shift_right_logical(rem_row_ref[g : g + 1, :], 9) for g in range(groups)]

    all_bytes(ra_ref.at[pl.ds(0, rows - 1)], recv_sems.at[0]).wait()
    own_src = lax.shift_right_logical(rem_col_ref[pl.ds(r * share, share), :], 10)
    strip = jnp.zeros((share, LANES), jnp.float32)
    for k in range(rows):
        strip = jnp.where(own_src == k, ra_ref[k], strip)
    for j in range(share):
        sb_ref[j] = strip[j : j + 1, :]
    spread_cols(lambda to: sb_ref.at[to], rb_ref.at[c], 2, cols)
    rb_ref[c] = sb_ref[c]

    all_bytes(ru_ref.at[pl.ds(0, rows - 1)], recv_sems.at[1]).wait()
    for g in range(groups):
        part = jnp.zeros((share, LANES), jnp.float32)
        src = lax.shift_right_logical(tile_row[g], 1)
        for k in range(rows):
            part = jnp.where(src == k, ru_ref[k], part)
        upper_ref[pl.ds(r * share, share), g * LANES : (g + 1) * LANES] = part

    all_bytes(rb_ref.at[pl.ds(0, cols - 1)], recv_sems.at[2]).wait()
    for g in range(groups):
        part = jnp.zeros((1, LANES), jnp.float32)
        for k in range(cols):
            part = jnp.where(tile_row[g] == k, rb_ref[k], part)
        row_ref[:, g * LANES : (g + 1) * LANES] = part
    spread_cols(lambda to: row_ref, rc_ref.at[c], 3, cols)
    rc_ref[c] = row_ref[...]

    spread_cols(lambda to: xh_ref.at[pl.ds(to * (share // 2), share // 2)], rl_ref.at[c], 4, cols)
    rl_ref[c] = xh_ref[pl.ds(c * (share // 2), share // 2), :]
    spread_cols(lambda to: xw_ref.at[pl.ds(to * wchunk, wchunk)], rw_ref.at[c], 5, wowners)

    all_bytes(rc_ref.at[pl.ds(0, cols - 1)], recv_sems.at[3]).wait()
    for j in range(share):
        block_ref[pl.ds(r * share + j, 1), :] = rc_ref[j]
    own_share = pl.ds(r * share, share)
    spread_rows(lambda to: block_ref.at[own_share], block_ref.at[own_share], 6)
    spread_rows(lambda to: upper_ref.at[own_share], upper_ref.at[own_share], 7)

    all_bytes(rl_ref.at[pl.ds(0, cols - 1)], recv_sems.at[4]).wait()
    first = lax.broadcasted_iota(jnp.int32, (share // 2, LANES), 1) < half
    for g in range(groups):
        turned = pltpu.roll(jnp.broadcast_to(tile_row[g], (8, LANES)), half, 1)[0:1, :]

        def gather_left(k, carry):
            straight, cross = carry
            x = rl_ref[k]
            return (
                jnp.where(tile_row[g] == k, x, straight),
                jnp.where(turned == k, x, cross),
            )

        zero = jnp.zeros((share // 2, LANES), jnp.float32)
        straight, cross = lax.fori_loop(0, cols, gather_left, (zero, zero))
        cross = pltpu.roll(cross, half, 1)
        where = slice(g * LANES, (g + 1) * LANES)
        left_ref[pl.ds(c * share, share // 2), where] = jnp.where(first, straight, cross)
        left_ref[pl.ds(c * share + share // 2, share // 2), where] = jnp.where(
            first, cross, straight
        )

    @pl.when(c < wowners)
    def _():
        rw_ref[c] = xw_ref[pl.ds(pl.multiple_of(c * wchunk, wchunk), wchunk), :]
        all_bytes(rw_ref.at[pl.ds(0, cols - 1)], recv_sems.at[5]).wait()
        for g in range(groups):

            def gather_weight(k, part):
                return jnp.where(tile_row[g] == k, rw_ref[k].astype(jnp.float32), part)

            wleft_ref[
                pl.ds(pl.multiple_of(c * wchunk, wchunk), wchunk), g * LANES : (g + 1) * LANES
            ] = lax.fori_loop(0, cols, gather_weight, jnp.zeros((wchunk, LANES), jnp.float32)).astype(
                jnp.bfloat16
            )

    sibling = c + 1 - 2 * lax.rem(c, 2)
    parity = lax.rem(c, 2)
    z = c // 2
    wz = wowners // 2
    plus, minus = zs // 2, zs - 1 - zs // 2
    sib_plus, sib_minus = 2, 3
    away = lax.rem(z + 1, zs), lax.rem(z + zs - 1, zs)

    bases = (0, plus, plus + minus, plus + minus + sib_plus, zs + sib_plus + sib_minus - 1)
    bases += (bases[4] + plus - sib_plus + 1 - sib_minus - 1,)

    def shares(z_src, side, kind, step, to, go):
        slot = 2 * z_src + side
        at = pl.ds(slot * share, share)
        at_sem = bases[kind] + (jnp.maximum(step - sib_plus, 0) if kind == 4 else step)
        go(
            pltpu.make_async_remote_copy(
                src_ref=left_ref.at[at],
                dst_ref=left_ref.at[at],
                send_sem=ring_send.at[at_sem],
                recv_sem=ring_recv.at[at_sem],
                device_id={"col": to},
                device_id_type=MESH,
            )
        )

        @pl.when(z_src < wz)
        def _():
            wat = pl.ds(pl.multiple_of(slot * wchunk, wchunk), wchunk)
            go(
                pltpu.make_async_remote_copy(
                    src_ref=wleft_ref.at[wat],
                    dst_ref=wleft_ref.at[wat],
                    send_sem=wring_send.at[at_sem],
                    recv_sem=wring_recv.at[at_sem],
                    device_id={"col": to},
                    device_id_type=MESH,
                )
            )

    start, recv, sent = (lambda d: d.start()), (lambda d: d.wait_recv()), (lambda d: d.wait_send())

    def behind(s):
        return lax.rem(z + zs - s, zs)

    def before(s):
        return lax.rem(z + s, zs)

    def send_own(s, go):
        @pl.when(s < plus)
        def _():
            shares(behind(s), parity, 0, s, 2 * away[0] + parity, go)

        @pl.when(s < minus)
        def _():
            shares(before(s), parity, 1, s, 2 * away[1] + parity, go)

        @pl.when((s == 0) | ((s > sib_plus) & (s <= plus)))
        def _():
            shares(behind(s), parity, 4, s, sibling, go)

        @pl.when((s > sib_minus) & (s <= minus))
        def _():
            shares(before(s), parity, 5, s, sibling, go)

    def send_other(s, go):
        @pl.when(s < sib_plus)
        def _():
            shares(behind(s), 1 - parity, 2, s, 2 * away[0] + parity, go)

        @pl.when(s < sib_minus)
        def _():
            shares(before(s), 1 - parity, 3, s, 2 * away[1] + parity, go)

    def ring_begin():
        send_own(0, start)
        shares(z, 1 - parity, 4, 0, sibling, recv)
        send_other(0, start)

    def ring_step(s):
        @pl.when(s <= plus)
        def _():
            shares(behind(s), parity, 0, s - 1, sibling, recv)

        @pl.when(s <= minus)
        def _():
            shares(before(s), parity, 1, s - 1, sibling, recv)

        send_own(s, start)

        @pl.when(s <= sib_plus)
        def _():
            shares(behind(s), 1 - parity, 2, s - 1, sibling, recv)

        @pl.when(s <= sib_minus)
        def _():
            shares(before(s), 1 - parity, 3, s - 1, sibling, recv)

        send_other(s, start)

    def ring_end():
        @pl.loop(sib_plus + 1, plus + 1)
        def _(s):
            shares(behind(s), 1 - parity, 4, s, sibling, recv)

            @pl.when((s > sib_minus) & (s <= minus))
            def _():
                shares(before(s), 1 - parity, 5, s, sibling, recv)

    def ring_sent():
        @pl.loop(0, plus + 1)
        def _(s):
            send_own(s, sent)
            send_other(s, sent)

    ring_begin()

    all_rows = pl.ds(0, (rows - 1) * share)
    all_bytes(block_ref.at[all_rows], recv_sems.at[6]).wait()
    all_bytes(block_ref.at[all_rows], send_sems.at[6]).wait()

    def invert_step(k, carry):
        at = pl.ds(pl.multiple_of(k * LANES, LANES), LANES)
        inverse = invert_tile(block_ref[at, at])
        ring_step(2 * k + 1)
        strip_ref[...] = dot6(inverse, block_ref[at, :])
        strip_ref[:, at] = inverse
        column = block_ref[:, at]
        block_ref[:, at] = jnp.zeros((count, LANES), jnp.float32)
        block_ref[...] -= dot6(column, strip_ref[...])
        block_ref[at, :] = strip_ref[...]
        ring_step(2 * k + 2)
        return carry

    lax.fori_loop(0, groups, invert_step, 0)

    all_bytes(upper_ref.at[all_rows], recv_sems.at[7]).wait()
    coupling_ref[...] = dot6(block_ref[...], upper_ref[...], b_dim=1)
    ring_end()

    all_bytes(ra_ref.at[pl.ds(0, rows - 1)], send_sems.at[0]).wait()
    all_bytes(ru_ref.at[pl.ds(0, rows - 1)], send_sems.at[1]).wait()
    all_bytes(rb_ref.at[pl.ds(0, cols - 1)], send_sems.at[2]).wait()
    all_bytes(rc_ref.at[pl.ds(0, cols - 1)], send_sems.at[3]).wait()
    all_bytes(rl_ref.at[pl.ds(0, cols - 1)], send_sems.at[4]).wait()

    @pl.when(c < wowners)
    def _():
        all_bytes(rw_ref.at[pl.ds(0, wowners - 1)], send_sems.at[5]).wait()

    @pl.when(c >= wowners)
    def _():
        all_bytes(rw_ref.at[pl.ds(0, wowners)], send_sems.at[5]).wait()

    all_bytes(upper_ref.at[all_rows], send_sems.at[7]).wait()
    ring_sent()


def exchange(hess_inv, weights, removed):
    rows, cols = lax.axis_size("row"), lax.axis_size("col")
    tall, wide = hess_inv.shape
    count = removed.shape[0]
    share = count // rows
    zs = cols // 2
    vmem = pl.BlockSpec(memory_space=pltpu.VMEM)
    f32, bf16 = jnp.float32, jnp.bfloat16
    dma = pltpu.SemaphoreType.DMA
    return pl.pallas_call(
        functools.partial(exchange_kernel, rows, cols),
        out_shape=(
            jax.ShapeDtypeStruct((count, wide), f32),
            jax.ShapeDtypeStruct((tall, count), f32),
            jax.ShapeDtypeStruct((weights.shape[0], count), bf16),
        ),
        in_specs=[vmem] * 4,
        out_specs=(vmem,) * 3,
        scratch_shapes=[
            pltpu.VMEM((count, count), f32),
            pltpu.VMEM((wide, count), f32),
            pltpu.VMEM((LANES, count), f32),
            pltpu.VMEM((wide, LANES), f32),
            pltpu.VMEM((LANES, LANES), f32),
            pltpu.VMEM((tall // 2, LANES), f32),
            pltpu.VMEM((weights.shape[0], LANES), bf16),
            pltpu.VMEM((rows, share, LANES), f32),
            pltpu.VMEM((rows, share, LANES), f32),
            pltpu.VMEM((share, 1, LANES), f32),
            pltpu.VMEM((cols, 1, LANES), f32),
            pltpu.VMEM((1, count), f32),
            pltpu.VMEM((cols, 1, count), f32),
            pltpu.VMEM((cols, share // 2, LANES), f32),
            pltpu.VMEM((cols, 16, LANES), bf16),
            dma((8,)),
            dma((8,)),
            dma((2 * zs,)),
            dma((2 * zs,)),
            dma((2 * zs,)),
            dma((2 * zs,)),
        ],
        compiler_params=pltpu.CompilerParams(
            collective_id=0, has_side_effects=True, vmem_limit_bytes=48 * 1024 * 1024
        ),
        cost_estimate=pl.CostEstimate(
            flops=2 * tall * wide * LANES * 6, bytes_accessed=8 * 1024 * 1024, transcendentals=0
        ),
        name="exchange",
    )(hess_inv, weights, removed.reshape(count // LANES, LANES), removed.reshape(count, 1))


def on_device(hess_inv, weights, removed):
    coupling, left, weight_left = exchange(hess_inv, weights, removed)
    hess_out = hess_inv - jnp.dot(left, coupling, precision=HIGHEST)
    weight_fix = jnp.dot(weight_left.astype(jnp.float32), coupling, precision=HIGHEST)
    weight_out = (weights.astype(jnp.float32) - weight_fix).astype(jnp.bfloat16)
    return (hess_out, weight_out)


def solution(mesh):
    placed = (P("row", "col"), P("row", "col"), P())
    return jax.shard_map(
        on_device,
        mesh=mesh,
        in_specs=placed,
        out_specs=(P("row", "col"), P("row", "col")),
        check_vma=False,
    )
```

```python
import functools

import jax
import jax.numpy as jnp
from jax import lax
from jax.experimental import pallas as pl
from jax.experimental.pallas import tpu as pltpu
from jax.sharding import PartitionSpec as P

MESH = pl.DeviceIdType.MESH
HIGHEST = lax.Precision.HIGHEST
LANES = 128


def all_bytes(ref, sem):
    return pltpu.make_async_copy(ref, ref, sem)


def split3(x):
    high = x.astype(jnp.bfloat16)
    rest = x - high.astype(jnp.float32)
    mid = rest.astype(jnp.bfloat16)
    return high, mid, (rest - mid.astype(jnp.float32)).astype(jnp.bfloat16)


def dot6(a, b, b_dim=0):
    ah, am, al = split3(a)
    bh, bm, bl = split3(b)
    return lax.dot_general(
        jnp.concatenate([ah, al, am, am, ah, ah], axis=1),
        jnp.concatenate([bl, bh, bm, bh, bm, bh], axis=b_dim),
        (((1,), (b_dim,)), ((), ())),
        preferred_element_type=jnp.float32,
    )


def eliminate(columns, panel):
    count = len(columns)
    sub = lax.broadcasted_iota(jnp.int32, (8, LANES), 0)

    def row(x, j):
        return jnp.broadcast_to(x[j // 8][j % 8 : j % 8 + 1, :], (8, LANES))

    todo = [list(x) for x in columns] + [list(panel)]
    for j in range(count):
        pivot = todo.pop(0)
        scale = 1.0 / row(pivot, j)
        for x in todo:
            new = row(x, j) * scale
            for t in range(len(x)):
                x[t] = x[t] - pivot[t] * new
            x[j // 8] = jnp.where(sub == j % 8, new, x[j // 8])
    return todo[0]


def invert_tile(tile):
    count = tile.shape[0] // 8
    v = [tile[8 * i : 8 * i + 8, :] for i in range(count)]
    lane = lax.broadcasted_iota(jnp.int32, (8, LANES), 1)
    sub = lax.broadcasted_iota(jnp.int32, (8, LANES), 0)

    def column(x, k):
        return jnp.broadcast_to(x[:, k : k + 1], (8, LANES))

    for b in range(count // 2):
        k = 16 * b
        rows = [2 * b, 2 * b + 1]
        ahead = [i for i in (2 * b + 2, 2 * b + 3) if i < count]
        rest = [i for i in range(count) if i not in rows and i not in ahead]
        inside = (lane >= k) & (lane < k + 16)
        columns = [[column(v[i], k + q) for i in rows] for q in range(16)]
        panel = [jnp.where(inside, jnp.where(lane == sub + 8 * i, 1.0, 0.0), v[i]) for i in rows]
        new = eliminate(columns, panel)
        w = list(v)
        for i in ahead:
            terms = [
                column(v[i], k + q)
                * jnp.broadcast_to(new[q // 8][q % 8 : q % 8 + 1, :], (8, LANES))
                for q in range(16)
            ]
            while len(terms) > 1:
                terms = [terms[z] + terms[z + 1] for z in range(0, len(terms), 2)]
            w[i] = jnp.where(inside, 0.0, v[i]) - terms[0]
        for t, i in enumerate(rows):
            w[i] = new[t]
        change = jnp.dot(
            jnp.concatenate([v[i] for i in rest], axis=0)[:, k : k + 16],
            jnp.concatenate(new, axis=0),
            precision=HIGHEST,
            preferred_element_type=jnp.float32,
        )
        for z, i in enumerate(rest):
            w[i] = jnp.where(inside, 0.0, v[i]) - change[8 * z : 8 * z + 8]
        v = w
    return jnp.concatenate(v, axis=0)


def exchange_kernel(
    rows,
    cols,
    hess_hbm,
    weight_hbm,
    rem_row_ref,
    coupling_ref,
    left_ref,
    wleft_ref,
    hess_ref,
    weight_ref,
    rem_col_ref,
    load_sems,
    block_ref,
    upper_ref,
    strip_ref,
    yt_ref,
    bp_ref,
    xh_ref,
    xw_ref,
    ra_ref,
    ru_ref,
    sb_ref,
    rb_ref,
    row_ref,
    rc_ref,
    rl_ref,
    rw_ref,
    send_sems,
    recv_sems,
    ring_send,
    ring_recv,
    wring_send,
    wring_recv,
):
    r = lax.axis_index("row")
    c = lax.axis_index("col")
    tall, wide = hess_ref.shape
    count = rem_col_ref.shape[0]
    groups = count // LANES
    share = count // rows
    zs = cols // 2
    wchunk = 16
    wowners = weight_ref.shape[0] // wchunk

    loads = [
        pltpu.make_async_copy(hess_hbm, hess_ref, load_sems.at[0]),
        pltpu.make_async_copy(weight_hbm, weight_ref, load_sems.at[1]),
    ]
    for load in loads:
        load.start()
    barrier = pltpu.get_barrier_semaphore()

    @pl.loop(1, rows)
    def _(k):
        pl.semaphore_signal(
            barrier, inc=1, device_id={"row": lax.rem(r + k, rows)}, device_id_type=MESH
        )

    @pl.loop(1, cols)
    def _(k):
        pl.semaphore_signal(
            barrier, inc=1, device_id={"col": lax.rem(c + k, cols)}, device_id_type=MESH
        )

    for g in range(groups):
        rem_col_ref[g * LANES : (g + 1) * LANES, :] = jnp.broadcast_to(
            rem_row_ref[g : g + 1, :], (LANES, LANES)
        ).T

    col_iota = lax.broadcasted_iota(jnp.int32, (wide, LANES), 0) + c * wide
    row_iota = lax.broadcasted_iota(jnp.int32, (LANES, tall), 1) + r * tall
    pick_col = jnp.zeros((wide, LANES), jnp.float32)
    pick_row = jnp.zeros((LANES, tall), jnp.float32)
    for g in range(groups):
        pick_col = jnp.where(rem_row_ref[g : g + 1, :] == col_iota, 1.0, pick_col)
        pick_row = jnp.where(
            rem_col_ref[g * LANES : (g + 1) * LANES, 0:1] == row_iota, 1.0, pick_row
        )

    for load in loads:
        load.wait()
    own_rows = jnp.dot(
        pick_row, hess_ref[...], precision=HIGHEST, preferred_element_type=jnp.float32
    )
    bp_ref[...] = jnp.dot(
        own_rows, pick_col, precision=HIGHEST, preferred_element_type=jnp.float32
    )
    pl.semaphore_wait(barrier, rows + cols - 2)

    def spread_rows(src, dst, which):
        @pl.loop(1, rows)
        def _(k):
            to = lax.rem(r + k, rows)
            pltpu.make_async_remote_copy(
                src_ref=src(to),
                dst_ref=dst,
                send_sem=send_sems.at[which],
                recv_sem=recv_sems.at[which],
                device_id={"row": to},
                device_id_type=MESH,
            ).start()

    def spread_cols(src, dst, which, limit):
        @pl.loop(1, cols)
        def _(k):
            to = lax.rem(c + k, cols)

            @pl.when(to < limit)
            def _():
                pltpu.make_async_remote_copy(
                    src_ref=src(to),
                    dst_ref=dst,
                    send_sem=send_sems.at[which],
                    recv_sem=recv_sems.at[which],
                    device_id={"col": to},
                    device_id_type=MESH,
                ).start()

    spread_rows(lambda to: bp_ref.at[pl.ds(lax.rem(to, 4) * share, share)], ra_ref.at[r], 0)
    ra_ref[r] = bp_ref[pl.ds(lax.rem(r, 4) * share, share), :]
    yt_ref[...] = own_rows.T
    spread_rows(lambda to: yt_ref.at[pl.ds(to * share, share)], ru_ref.at[r], 1)
    ru_ref[r] = yt_ref[pl.ds(r * share, share), :]

    half = LANES // 2
    low = lax.broadcasted_iota(jnp.int32, (wide, LANES), 1) < half
    fold = pick_col + pltpu.roll(pick_col, half, 1)
    pick_half = jnp.concatenate(
        [jnp.where(low, fold, 0.0), jnp.where(low, 0.0, fold)], axis=0
    ).astype(jnp.bfloat16)
    parts = hess_ref[...].reshape(tall // share, 2, share // 2, wide)
    pairs = jnp.concatenate(
        [parts[:, 0].reshape(tall // 2, wide), parts[:, 1].reshape(tall // 2, wide)], axis=1
    )
    packed = [
        jnp.dot(x, pick_half, preferred_element_type=jnp.float32) for x in split3(pairs)
    ]
    xh_ref[...] = (packed[2] + packed[1]) + packed[0]
    xw_ref[...] = jnp.dot(
        weight_ref[...], pick_col.astype(jnp.bfloat16), preferred_element_type=jnp.float32
    ).astype(jnp.bfloat16)

    tile_row = [lax.shift_right_logical(rem_row_ref[g : g + 1, :], 9) for g in range(groups)]

    all_bytes(ra_ref.at[pl.ds(0, rows - 1)], recv_sems.at[0]).wait()
    own_src = lax.shift_right_logical(rem_col_ref[pl.ds(r * share, share), :], 10)
    strip = jnp.zeros((share, LANES), jnp.float32)
    for k in range(rows):
        strip = jnp.where(own_src == k, ra_ref[k], strip)
    for j in range(share):
        sb_ref[j] = strip[j : j + 1, :]
    spread_cols(lambda to: sb_ref.at[to], rb_ref.at[c], 2, cols)
    rb_ref[c] = sb_ref[c]

    all_bytes(ru_ref.at[pl.ds(0, rows - 1)], recv_sems.at[1]).wait()
    for g in range(groups):
        part = jnp.zeros((share, LANES), jnp.float32)
        src = lax.shift_right_logical(tile_row[g], 1)
        for k in range(rows):
            part = jnp.where(src == k, ru_ref[k], part)
        upper_ref[pl.ds(r * share, share), g * LANES : (g + 1) * LANES] = part

    own_share = pl.ds(r * share, share)
    spread_rows(lambda to: upper_ref.at[own_share], upper_ref.at[own_share], 7)

    all_bytes(rb_ref.at[pl.ds(0, cols - 1)], recv_sems.at[2]).wait()
    for g in range(groups):
        part = jnp.zeros((1, LANES), jnp.float32)
        for k in range(cols):
            part = jnp.where(tile_row[g] == k, rb_ref[k], part)
        row_ref[:, g * LANES : (g + 1) * LANES] = part
    spread_cols(lambda to: row_ref, rc_ref.at[c], 3, cols)
    rc_ref[c] = row_ref[...]

    spread_cols(lambda to: xh_ref.at[pl.ds(to * (share // 2), share // 2)], rl_ref.at[c], 4, cols)
    rl_ref[c] = xh_ref[pl.ds(c * (share // 2), share // 2), :]
    spread_cols(lambda to: xw_ref.at[pl.ds(to * wchunk, wchunk)], rw_ref.at[c], 5, wowners)

    all_bytes(rc_ref.at[pl.ds(0, cols - 1)], recv_sems.at[3]).wait()
    for j in range(share):
        block_ref[pl.ds(r * share + j, 1), :] = rc_ref[j]
    spread_rows(lambda to: block_ref.at[own_share], block_ref.at[own_share], 6)

    all_bytes(rl_ref.at[pl.ds(0, cols - 1)], recv_sems.at[4]).wait()
    first = lax.broadcasted_iota(jnp.int32, (share // 2, LANES), 1) < half
    for g in range(groups):
        turned = pltpu.roll(jnp.broadcast_to(tile_row[g], (8, LANES)), half, 1)[0:1, :]

        def gather_left(k, carry):
            straight, cross = carry
            x = rl_ref[k]
            return (
                jnp.where(tile_row[g] == k, x, straight),
                jnp.where(turned == k, x, cross),
            )

        zero = jnp.zeros((share // 2, LANES), jnp.float32)
        straight, cross = lax.fori_loop(0, cols, gather_left, (zero, zero))
        cross = pltpu.roll(cross, half, 1)
        where = slice(g * LANES, (g + 1) * LANES)
        left_ref[pl.ds(c * share, share // 2), where] = jnp.where(first, straight, cross)
        left_ref[pl.ds(c * share + share // 2, share // 2), where] = jnp.where(
            first, cross, straight
        )

    @pl.when(c < wowners)
    def _():
        rw_ref[c] = xw_ref[pl.ds(pl.multiple_of(c * wchunk, wchunk), wchunk), :]
        all_bytes(rw_ref.at[pl.ds(0, cols - 1)], recv_sems.at[5]).wait()
        for g in range(groups):

            def gather_weight(k, part):
                return jnp.where(tile_row[g] == k, rw_ref[k].astype(jnp.float32), part)

            wleft_ref[
                pl.ds(pl.multiple_of(c * wchunk, wchunk), wchunk), g * LANES : (g + 1) * LANES
            ] = lax.fori_loop(0, cols, gather_weight, jnp.zeros((wchunk, LANES), jnp.float32)).astype(
                jnp.bfloat16
            )

    sibling = c + 1 - 2 * lax.rem(c, 2)
    parity = lax.rem(c, 2)
    z = c // 2
    wz = wowners // 2
    plus, minus = zs // 2, zs - 1 - zs // 2
    sib_plus, sib_minus = 4, 5
    away = lax.rem(z + 1, zs), lax.rem(z + zs - 1, zs)

    bases = (0, plus, plus + minus, plus + minus + sib_plus, zs + sib_plus + sib_minus - 1)
    bases += (bases[4] + plus - sib_plus + 1 - sib_minus - 1,)

    def shares(z_src, side, kind, step, to, go):
        slot = 2 * z_src + side
        at = pl.ds(slot * share, share)
        at_sem = bases[kind] + (jnp.maximum(step - sib_plus, 0) if kind == 4 else step)
        go(
            pltpu.make_async_remote_copy(
                src_ref=left_ref.at[at],
                dst_ref=left_ref.at[at],
                send_sem=ring_send.at[at_sem],
                recv_sem=ring_recv.at[at_sem],
                device_id={"col": to},
                device_id_type=MESH,
            )
        )

        @pl.when(z_src < wz)
        def _():
            wat = pl.ds(pl.multiple_of(slot * wchunk, wchunk), wchunk)
            go(
                pltpu.make_async_remote_copy(
                    src_ref=wleft_ref.at[wat],
                    dst_ref=wleft_ref.at[wat],
                    send_sem=wring_send.at[at_sem],
                    recv_sem=wring_recv.at[at_sem],
                    device_id={"col": to},
                    device_id_type=MESH,
                )
            )

    start, recv, sent = (lambda d: d.start()), (lambda d: d.wait_recv()), (lambda d: d.wait_send())

    def behind(s):
        return lax.rem(z + zs - s, zs)

    def before(s):
        return lax.rem(z + s, zs)

    def send_own(s, go):
        @pl.when(s < plus)
        def _():
            shares(behind(s), parity, 0, s, 2 * away[0] + parity, go)

        @pl.when(s < minus)
        def _():
            shares(before(s), parity, 1, s, 2 * away[1] + parity, go)

        @pl.when((s == 0) | ((s > sib_plus) & (s <= plus)))
        def _():
            shares(behind(s), parity, 4, s, sibling, go)

        @pl.when((s > sib_minus) & (s <= minus))
        def _():
            shares(before(s), parity, 5, s, sibling, go)

    def send_other(s, go):
        @pl.when(s < sib_plus)
        def _():
            shares(behind(s), 1 - parity, 2, s, 2 * away[0] + parity, go)

        @pl.when(s < sib_minus)
        def _():
            shares(before(s), 1 - parity, 3, s, 2 * away[1] + parity, go)

    def ring_begin():
        send_own(0, start)
        shares(z, 1 - parity, 4, 0, sibling, recv)
        send_other(0, start)

    def ring_step(s):
        @pl.when(s <= plus)
        def _():
            shares(behind(s), parity, 0, s - 1, sibling, recv)

        @pl.when(s <= minus)
        def _():
            shares(before(s), parity, 1, s - 1, sibling, recv)

        send_own(s, start)

        @pl.when(s <= sib_plus)
        def _():
            shares(behind(s), 1 - parity, 2, s - 1, sibling, recv)

        @pl.when(s <= sib_minus)
        def _():
            shares(before(s), 1 - parity, 3, s - 1, sibling, recv)

        send_other(s, start)

    def ring_end():
        @pl.loop(sib_plus + 1, plus + 1)
        def _(s):
            shares(behind(s), 1 - parity, 4, s, sibling, recv)

            @pl.when((s > sib_minus) & (s <= minus))
            def _():
                shares(before(s), 1 - parity, 5, s, sibling, recv)

    def ring_sent():
        @pl.loop(0, plus + 1)
        def _(s):
            send_own(s, sent)
            send_other(s, sent)

    ring_begin()

    all_rows = pl.ds(0, (rows - 1) * share)
    all_bytes(block_ref.at[all_rows], recv_sems.at[6]).wait()
    all_bytes(block_ref.at[all_rows], send_sems.at[6]).wait()

    def invert_step(k, carry):
        at = pl.ds(pl.multiple_of(k * LANES, LANES), LANES)
        inverse = invert_tile(block_ref[at, at])
        ring_step(2 * k + 1)
        strip_ref[...] = dot6(inverse, block_ref[at, :])
        strip_ref[:, at] = inverse
        column = block_ref[:, at]
        block_ref[:, at] = jnp.zeros((count, LANES), jnp.float32)
        block_ref[...] -= dot6(column, strip_ref[...])
        block_ref[at, :] = strip_ref[...]
        ring_step(2 * k + 2)
        return carry

    lax.fori_loop(0, groups, invert_step, 0)

    all_bytes(upper_ref.at[all_rows], recv_sems.at[7]).wait()
    coupling_ref[...] = dot6(block_ref[...], upper_ref[...], b_dim=1)
    ring_end()

    all_bytes(ra_ref.at[pl.ds(0, rows - 1)], send_sems.at[0]).wait()
    all_bytes(ru_ref.at[pl.ds(0, rows - 1)], send_sems.at[1]).wait()
    all_bytes(rb_ref.at[pl.ds(0, cols - 1)], send_sems.at[2]).wait()
    all_bytes(rc_ref.at[pl.ds(0, cols - 1)], send_sems.at[3]).wait()
    all_bytes(rl_ref.at[pl.ds(0, cols - 1)], send_sems.at[4]).wait()

    @pl.when(c < wowners)
    def _():
        all_bytes(rw_ref.at[pl.ds(0, wowners - 1)], send_sems.at[5]).wait()

    @pl.when(c >= wowners)
    def _():
        all_bytes(rw_ref.at[pl.ds(0, wowners)], send_sems.at[5]).wait()

    all_bytes(upper_ref.at[all_rows], send_sems.at[7]).wait()
    ring_sent()


def exchange(hess_inv, weights, removed):
    rows, cols = lax.axis_size("row"), lax.axis_size("col")
    tall, wide = hess_inv.shape
    count = removed.shape[0]
    share = count // rows
    zs = cols // 2
    vmem = pl.BlockSpec(memory_space=pltpu.VMEM)
    f32, bf16 = jnp.float32, jnp.bfloat16
    dma = pltpu.SemaphoreType.DMA
    return pl.pallas_call(
        functools.partial(exchange_kernel, rows, cols),
        out_shape=(
            jax.ShapeDtypeStruct((count, wide), f32),
            jax.ShapeDtypeStruct((tall, count), f32),
            jax.ShapeDtypeStruct((weights.shape[0], count), bf16),
        ),
        in_specs=[pl.BlockSpec(memory_space=pl.ANY)] * 2 + [vmem],
        out_specs=(vmem,) * 3,
        scratch_shapes=[
            pltpu.VMEM((tall, wide), f32),
            pltpu.VMEM(weights.shape, bf16),
            pltpu.VMEM((count, LANES), jnp.int32),
            dma((2,)),
            pltpu.VMEM((count, count), f32),
            pltpu.VMEM((wide, count), f32),
            pltpu.VMEM((LANES, count), f32),
            pltpu.VMEM((wide, LANES), f32),
            pltpu.VMEM((LANES, LANES), f32),
            pltpu.VMEM((tall // 2, LANES), f32),
            pltpu.VMEM((weights.shape[0], LANES), bf16),
            pltpu.VMEM((rows, share, LANES), f32),
            pltpu.VMEM((rows, share, LANES), f32),
            pltpu.VMEM((share, 1, LANES), f32),
            pltpu.VMEM((cols, 1, LANES), f32),
            pltpu.VMEM((1, count), f32),
            pltpu.VMEM((cols, 1, count), f32),
            pltpu.VMEM((cols, share // 2, LANES), f32),
            pltpu.VMEM((cols, 16, LANES), bf16),
            dma((8,)),
            dma((8,)),
            dma((2 * zs,)),
            dma((2 * zs,)),
            dma((2 * zs,)),
            dma((2 * zs,)),
        ],
        compiler_params=pltpu.CompilerParams(
            collective_id=0, has_side_effects=True, vmem_limit_bytes=48 * 1024 * 1024
        ),
        cost_estimate=pl.CostEstimate(
            flops=2 * tall * wide * LANES * 6, bytes_accessed=8 * 1024 * 1024, transcendentals=0
        ),
        name="exchange",
    )(hess_inv, weights, removed.reshape(count // LANES, LANES))


def update_kernel(
    hess_ref, weight_ref, left_ref, wleft_ref, coupling_ref, hess_out_ref, weight_out_ref, terms_ref
):
    count = coupling_ref.shape[0]

    @pl.when(pl.program_id(0) == 0)
    def _():
        high, mid, _ = split3(coupling_ref[...])
        terms_ref[0:count] = high
        terms_ref[count : 2 * count] = mid
        terms_ref[2 * count : 3 * count] = high

    high, mid, _ = split3(left_ref[...])
    hess_out_ref[...] = hess_ref[...] - jnp.dot(
        jnp.concatenate([mid, high, high], axis=1),
        terms_ref[...],
        preferred_element_type=jnp.float32,
    )
    own = wleft_ref[...]
    change = jnp.dot(
        jnp.concatenate([own, own], axis=1),
        terms_ref[count : 3 * count],
        preferred_element_type=jnp.float32,
    )
    weight_out_ref[...] = (weight_ref[...].astype(jnp.float32) - change).astype(jnp.bfloat16)


def update(hess_inv, weights, left, weight_left, coupling):
    steps = 4
    count, wide = coupling.shape
    tall, high = hess_inv.shape[0] // steps, weights.shape[0] // steps

    def rows_of(size, width):
        return pl.BlockSpec((size, width), lambda i: (i, 0))

    return pl.pallas_call(
        update_kernel,
        grid=(steps,),
        out_shape=(
            jax.ShapeDtypeStruct(hess_inv.shape, jnp.float32),
            jax.ShapeDtypeStruct(weights.shape, jnp.bfloat16),
        ),
        in_specs=[
            rows_of(tall, wide),
            rows_of(high, wide),
            rows_of(tall, count),
            rows_of(high, count),
            pl.BlockSpec((count, wide), lambda i: (0, 0)),
        ],
        out_specs=(rows_of(tall, wide), rows_of(high, wide)),
        scratch_shapes=[pltpu.VMEM((3 * count, wide), jnp.bfloat16)],
        compiler_params=pltpu.CompilerParams(vmem_limit_bytes=32 * 1024 * 1024),
        name="update",
    )(hess_inv, weights, left, weight_left, coupling)


def on_device(hess_inv, weights, removed):
    coupling, left, weight_left = exchange(hess_inv, weights, removed)
    return update(hess_inv, weights, left, weight_left, coupling)


def solution(mesh):
    placed = (P("row", "col"), P("row", "col"), P())
    return jax.shard_map(
        on_device,
        mesh=mesh,
        in_specs=placed,
        out_specs=(P("row", "col"), P("row", "col")),
        check_vma=False,
    )
```

```python
import functools

import jax
import jax.numpy as jnp
from jax import lax
from jax.experimental import pallas as pl
from jax.experimental.pallas import tpu as pltpu
from jax.sharding import PartitionSpec as P

MESH = pl.DeviceIdType.MESH
HIGHEST = lax.Precision.HIGHEST
LANES = 128


def all_bytes(ref, sem):
    return pltpu.make_async_copy(ref, ref, sem)


def split3(x):
    high = x.astype(jnp.bfloat16)
    rest = x - high.astype(jnp.float32)
    mid = rest.astype(jnp.bfloat16)
    return high, mid, (rest - mid.astype(jnp.float32)).astype(jnp.bfloat16)


def dot6(a, b, b_dim=0):
    ah, am, al = split3(a)
    bh, bm, bl = split3(b)
    return lax.dot_general(
        jnp.concatenate([ah, al, am, am, ah, ah], axis=1),
        jnp.concatenate([bl, bh, bm, bh, bm, bh], axis=b_dim),
        (((1,), (b_dim,)), ((), ())),
        preferred_element_type=jnp.float32,
    )


def eliminate(columns, panel):
    count = len(columns)
    sub = lax.broadcasted_iota(jnp.int32, (8, LANES), 0)

    def row(x, j):
        return jnp.broadcast_to(x[j // 8][j % 8 : j % 8 + 1, :], (8, LANES))

    todo = [list(x) for x in columns] + [list(panel)]
    for j in range(count):
        pivot = todo.pop(0)
        scale = 1.0 / row(pivot, j)
        for x in todo:
            new = row(x, j) * scale
            for t in range(len(x)):
                x[t] = x[t] - pivot[t] * new
            x[j // 8] = jnp.where(sub == j % 8, new, x[j // 8])
    return todo[0]


def invert_tile(tile):
    count = tile.shape[0] // 8
    v = [tile[8 * i : 8 * i + 8, :] for i in range(count)]
    lane = lax.broadcasted_iota(jnp.int32, (8, LANES), 1)
    sub = lax.broadcasted_iota(jnp.int32, (8, LANES), 0)

    def column(x, k):
        return jnp.broadcast_to(x[:, k : k + 1], (8, LANES))

    for b in range(count // 2):
        k = 16 * b
        rows = [2 * b, 2 * b + 1]
        ahead = [i for i in (2 * b + 2, 2 * b + 3) if i < count]
        rest = [i for i in range(count) if i not in rows and i not in ahead]
        inside = (lane >= k) & (lane < k + 16)
        columns = [[column(v[i], k + q) for i in rows] for q in range(16)]
        panel = [jnp.where(inside, jnp.where(lane == sub + 8 * i, 1.0, 0.0), v[i]) for i in rows]
        new = eliminate(columns, panel)
        w = list(v)
        for i in ahead:
            terms = [
                column(v[i], k + q)
                * jnp.broadcast_to(new[q // 8][q % 8 : q % 8 + 1, :], (8, LANES))
                for q in range(16)
            ]
            while len(terms) > 1:
                terms = [terms[z] + terms[z + 1] for z in range(0, len(terms), 2)]
            w[i] = jnp.where(inside, 0.0, v[i]) - terms[0]
        for t, i in enumerate(rows):
            w[i] = new[t]
        change = jnp.dot(
            jnp.concatenate([v[i] for i in rest], axis=0)[:, k : k + 16],
            jnp.concatenate(new, axis=0),
            precision=HIGHEST,
            preferred_element_type=jnp.float32,
        )
        for z, i in enumerate(rest):
            w[i] = jnp.where(inside, 0.0, v[i]) - change[8 * z : 8 * z + 8]
        v = w
    return jnp.concatenate(v, axis=0)


def exchange_kernel(
    rows,
    cols,
    hess_hbm,
    weight_hbm,
    rem_row_ref,
    coupling_ref,
    left_ref,
    wleft_ref,
    hess_ref,
    weight_ref,
    rem_col_ref,
    load_sems,
    block_ref,
    upper_ref,
    strip_ref,
    yt_ref,
    bp_ref,
    xh_ref,
    xw_ref,
    ra_ref,
    ru_ref,
    sb_ref,
    rb_ref,
    row_ref,
    rc_ref,
    rl_ref,
    rw_ref,
    send_sems,
    recv_sems,
    ring_send,
    ring_recv,
    wring_send,
    wring_recv,
):
    r = lax.axis_index("row")
    c = lax.axis_index("col")
    tall, wide = hess_ref.shape
    count = rem_col_ref.shape[0]
    groups = count // LANES
    share = count // rows
    zs = cols // 2
    wchunk = 16
    wowners = weight_ref.shape[0] // wchunk

    loads = [
        pltpu.make_async_copy(hess_hbm, hess_ref, load_sems.at[0]),
        pltpu.make_async_copy(weight_hbm, weight_ref, load_sems.at[1]),
    ]
    for load in loads:
        load.start()
    barrier = pltpu.get_barrier_semaphore()

    @pl.loop(1, rows)
    def _(k):
        pl.semaphore_signal(
            barrier, inc=1, device_id={"row": lax.rem(r + k, rows)}, device_id_type=MESH
        )

    @pl.loop(1, cols)
    def _(k):
        pl.semaphore_signal(
            barrier, inc=1, device_id={"col": lax.rem(c + k, cols)}, device_id_type=MESH
        )

    for g in range(groups):
        rem_col_ref[g * LANES : (g + 1) * LANES, :] = jnp.broadcast_to(
            rem_row_ref[g : g + 1, :], (LANES, LANES)
        ).T

    col_iota = lax.broadcasted_iota(jnp.int32, (wide, LANES), 0) + c * wide
    row_iota = lax.broadcasted_iota(jnp.int32, (LANES, tall), 1) + r * tall
    pick_col = jnp.zeros((wide, LANES), jnp.float32)
    pick_row = jnp.zeros((LANES, tall), jnp.float32)
    for g in range(groups):
        pick_col = jnp.where(rem_row_ref[g : g + 1, :] == col_iota, 1.0, pick_col)
        pick_row = jnp.where(
            rem_col_ref[g * LANES : (g + 1) * LANES, 0:1] == row_iota, 1.0, pick_row
        )

    for load in loads:
        load.wait()
    own_rows = jnp.dot(
        pick_row, hess_ref[...], precision=HIGHEST, preferred_element_type=jnp.float32
    )
    bp_ref[...] = jnp.dot(
        own_rows, pick_col, precision=HIGHEST, preferred_element_type=jnp.float32
    )
    pl.semaphore_wait(barrier, rows + cols - 2)

    def spread_rows(src, dst, which):
        @pl.loop(1, rows)
        def _(k):
            to = lax.rem(r + k, rows)
            pltpu.make_async_remote_copy(
                src_ref=src(to),
                dst_ref=dst,
                send_sem=send_sems.at[which],
                recv_sem=recv_sems.at[which],
                device_id={"row": to},
                device_id_type=MESH,
            ).start()

    def spread_cols(src, dst, which, limit):
        @pl.loop(1, cols)
        def _(k):
            to = lax.rem(c + k, cols)

            @pl.when(to < limit)
            def _():
                pltpu.make_async_remote_copy(
                    src_ref=src(to),
                    dst_ref=dst,
                    send_sem=send_sems.at[which],
                    recv_sem=recv_sems.at[which],
                    device_id={"col": to},
                    device_id_type=MESH,
                ).start()

    spread_rows(lambda to: bp_ref.at[pl.ds(lax.rem(to, 4) * share, share)], ra_ref.at[r], 0)
    ra_ref[r] = bp_ref[pl.ds(lax.rem(r, 4) * share, share), :]
    yt_ref[...] = own_rows.T
    spread_rows(lambda to: yt_ref.at[pl.ds(to * share, share)], ru_ref.at[r], 1)
    ru_ref[r] = yt_ref[pl.ds(r * share, share), :]

    half = LANES // 2
    low = lax.broadcasted_iota(jnp.int32, (wide, LANES), 1) < half
    fold = pick_col + pltpu.roll(pick_col, half, 1)
    pick_half = jnp.concatenate(
        [jnp.where(low, fold, 0.0), jnp.where(low, 0.0, fold)], axis=0
    ).astype(jnp.bfloat16)
    parts = hess_ref[...].reshape(tall // share, 2, share // 2, wide)
    pairs = jnp.concatenate(
        [parts[:, 0].reshape(tall // 2, wide), parts[:, 1].reshape(tall // 2, wide)], axis=1
    )
    packed = [
        jnp.dot(x, pick_half, preferred_element_type=jnp.float32) for x in split3(pairs)
    ]
    xh_ref[...] = (packed[2] + packed[1]) + packed[0]
    xw_ref[...] = jnp.dot(
        weight_ref[...], pick_col.astype(jnp.bfloat16), preferred_element_type=jnp.float32
    ).astype(jnp.bfloat16)

    tile_row = [lax.shift_right_logical(rem_row_ref[g : g + 1, :], 9) for g in range(groups)]

    all_bytes(ra_ref.at[pl.ds(0, rows - 1)], recv_sems.at[0]).wait()
    own_src = lax.shift_right_logical(rem_col_ref[pl.ds(r * share, share), :], 10)
    strip = jnp.zeros((share, LANES), jnp.float32)
    for k in range(rows):
        strip = jnp.where(own_src == k, ra_ref[k], strip)
    for j in range(share):
        sb_ref[j] = strip[j : j + 1, :]
    spread_cols(lambda to: sb_ref.at[to], rb_ref.at[c], 2, cols)
    rb_ref[c] = sb_ref[c]

    all_bytes(ru_ref.at[pl.ds(0, rows - 1)], recv_sems.at[1]).wait()
    for g in range(groups):
        part = jnp.zeros((share, LANES), jnp.float32)
        src = lax.shift_right_logical(tile_row[g], 1)
        for k in range(rows):
            part = jnp.where(src == k, ru_ref[k], part)
        upper_ref[pl.ds(r * share, share), g * LANES : (g + 1) * LANES] = part

    own_share = pl.ds(r * share, share)
    spread_rows(lambda to: upper_ref.at[own_share], upper_ref.at[own_share], 7)

    all_bytes(rb_ref.at[pl.ds(0, cols - 1)], recv_sems.at[2]).wait()
    for g in range(groups):
        part = jnp.zeros((1, LANES), jnp.float32)
        for k in range(cols):
            part = jnp.where(tile_row[g] == k, rb_ref[k], part)
        row_ref[:, g * LANES : (g + 1) * LANES] = part
    spread_cols(lambda to: row_ref, rc_ref.at[c], 3, cols)
    rc_ref[c] = row_ref[...]

    spread_cols(lambda to: xh_ref.at[pl.ds(to * (share // 2), share // 2)], rl_ref.at[c], 4, cols)
    rl_ref[c] = xh_ref[pl.ds(c * (share // 2), share // 2), :]
    spread_cols(lambda to: xw_ref.at[pl.ds(to * wchunk, wchunk)], rw_ref.at[c], 5, wowners)

    all_bytes(rc_ref.at[pl.ds(0, cols - 1)], recv_sems.at[3]).wait()
    for j in range(share):
        block_ref[pl.ds(r * share + j, 1), :] = rc_ref[j]
    spread_rows(lambda to: block_ref.at[own_share], block_ref.at[own_share], 6)

    all_bytes(rl_ref.at[pl.ds(0, cols - 1)], recv_sems.at[4]).wait()
    first = lax.broadcasted_iota(jnp.int32, (share // 2, LANES), 1) < half
    for g in range(groups):
        turned = pltpu.roll(jnp.broadcast_to(tile_row[g], (8, LANES)), half, 1)[0:1, :]

        def gather_left(k, carry):
            straight, cross = carry
            x = rl_ref[k]
            return (
                jnp.where(tile_row[g] == k, x, straight),
                jnp.where(turned == k, x, cross),
            )

        zero = jnp.zeros((share // 2, LANES), jnp.float32)
        straight, cross = lax.fori_loop(0, cols, gather_left, (zero, zero))
        cross = pltpu.roll(cross, half, 1)
        where = slice(g * LANES, (g + 1) * LANES)
        left_ref[pl.ds(c * share, share // 2), where] = jnp.where(first, straight, cross)
        left_ref[pl.ds(c * share + share // 2, share // 2), where] = jnp.where(
            first, cross, straight
        )

    @pl.when(c < wowners)
    def _():
        rw_ref[c] = xw_ref[pl.ds(pl.multiple_of(c * wchunk, wchunk), wchunk), :]
        all_bytes(rw_ref.at[pl.ds(0, cols - 1)], recv_sems.at[5]).wait()
        for g in range(groups):

            def gather_weight(k, part):
                return jnp.where(tile_row[g] == k, rw_ref[k].astype(jnp.float32), part)

            wleft_ref[
                pl.ds(pl.multiple_of(c * wchunk, wchunk), wchunk), g * LANES : (g + 1) * LANES
            ] = lax.fori_loop(0, cols, gather_weight, jnp.zeros((wchunk, LANES), jnp.float32)).astype(
                jnp.bfloat16
            )

    sibling = c + 1 - 2 * lax.rem(c, 2)
    parity = lax.rem(c, 2)
    z = c // 2
    wz = wowners // 2
    plus, minus = zs // 2, zs - 1 - zs // 2
    sib_plus, sib_minus = 4, 5
    away = lax.rem(z + 1, zs), lax.rem(z + zs - 1, zs)

    bases = (0, plus, plus + minus, plus + minus + sib_plus, zs + sib_plus + sib_minus - 1)
    bases += (bases[4] + plus - sib_plus + 1 - sib_minus - 1,)

    def shares(z_src, side, kind, step, to, go):
        slot = 2 * z_src + side
        at = pl.ds(slot * share, share)
        at_sem = bases[kind] + (jnp.maximum(step - sib_plus, 0) if kind == 4 else step)
        go(
            pltpu.make_async_remote_copy(
                src_ref=left_ref.at[at],
                dst_ref=left_ref.at[at],
                send_sem=ring_send.at[at_sem],
                recv_sem=ring_recv.at[at_sem],
                device_id={"col": to},
                device_id_type=MESH,
            )
        )

        @pl.when(z_src < wz)
        def _():
            wat = pl.ds(pl.multiple_of(slot * wchunk, wchunk), wchunk)
            go(
                pltpu.make_async_remote_copy(
                    src_ref=wleft_ref.at[wat],
                    dst_ref=wleft_ref.at[wat],
                    send_sem=wring_send.at[at_sem],
                    recv_sem=wring_recv.at[at_sem],
                    device_id={"col": to},
                    device_id_type=MESH,
                )
            )

    start, recv, sent = (lambda d: d.start()), (lambda d: d.wait_recv()), (lambda d: d.wait_send())

    def behind(s):
        return lax.rem(z + zs - s, zs)

    def before(s):
        return lax.rem(z + s, zs)

    def send_own(s, go):
        @pl.when(s < plus)
        def _():
            shares(behind(s), parity, 0, s, 2 * away[0] + parity, go)

        @pl.when(s < minus)
        def _():
            shares(before(s), parity, 1, s, 2 * away[1] + parity, go)

        @pl.when((s == 0) | ((s > sib_plus) & (s <= plus)))
        def _():
            shares(behind(s), parity, 4, s, sibling, go)

        @pl.when((s > sib_minus) & (s <= minus))
        def _():
            shares(before(s), parity, 5, s, sibling, go)

    def send_other(s, go):
        @pl.when(s < sib_plus)
        def _():
            shares(behind(s), 1 - parity, 2, s, 2 * away[0] + parity, go)

        @pl.when(s < sib_minus)
        def _():
            shares(before(s), 1 - parity, 3, s, 2 * away[1] + parity, go)

    def ring_begin():
        send_own(0, start)
        shares(z, 1 - parity, 4, 0, sibling, recv)
        send_other(0, start)

    def ring_step(s):
        @pl.when(s <= plus)
        def _():
            shares(behind(s), parity, 0, s - 1, sibling, recv)

        @pl.when(s <= minus)
        def _():
            shares(before(s), parity, 1, s - 1, sibling, recv)

        send_own(s, start)

        @pl.when(s <= sib_plus)
        def _():
            shares(behind(s), 1 - parity, 2, s - 1, sibling, recv)

        @pl.when(s <= sib_minus)
        def _():
            shares(before(s), 1 - parity, 3, s - 1, sibling, recv)

        send_other(s, start)

    def ring_end():
        @pl.loop(sib_plus + 1, plus + 1)
        def _(s):
            shares(behind(s), 1 - parity, 4, s, sibling, recv)

            @pl.when((s > sib_minus) & (s <= minus))
            def _():
                shares(before(s), 1 - parity, 5, s, sibling, recv)

    def ring_sent():
        @pl.loop(0, plus + 1)
        def _(s):
            send_own(s, sent)
            send_other(s, sent)

    ring_begin()

    all_rows = pl.ds(0, (rows - 1) * share)
    all_bytes(block_ref.at[all_rows], recv_sems.at[6]).wait()
    all_bytes(block_ref.at[all_rows], send_sems.at[6]).wait()

    def invert_step(k, carry):
        at = pl.ds(pl.multiple_of(k * LANES, LANES), LANES)
        inverse = invert_tile(block_ref[at, at])
        ring_step(2 * k + 1)
        strip_ref[...] = dot6(inverse, block_ref[at, :])
        strip_ref[:, at] = inverse
        column = block_ref[:, at]
        block_ref[:, at] = jnp.zeros((count, LANES), jnp.float32)
        block_ref[...] -= dot6(column, strip_ref[...])
        block_ref[at, :] = strip_ref[...]
        ring_step(2 * k + 2)
        return carry

    lax.fori_loop(0, groups, invert_step, 0)

    all_bytes(upper_ref.at[all_rows], recv_sems.at[7]).wait()
    coupling_ref[...] = dot6(block_ref[...], upper_ref[...], b_dim=1)
    ring_end()

    all_bytes(ra_ref.at[pl.ds(0, rows - 1)], send_sems.at[0]).wait()
    all_bytes(ru_ref.at[pl.ds(0, rows - 1)], send_sems.at[1]).wait()
    all_bytes(rb_ref.at[pl.ds(0, cols - 1)], send_sems.at[2]).wait()
    all_bytes(rc_ref.at[pl.ds(0, cols - 1)], send_sems.at[3]).wait()
    all_bytes(rl_ref.at[pl.ds(0, cols - 1)], send_sems.at[4]).wait()

    @pl.when(c < wowners)
    def _():
        all_bytes(rw_ref.at[pl.ds(0, wowners - 1)], send_sems.at[5]).wait()

    @pl.when(c >= wowners)
    def _():
        all_bytes(rw_ref.at[pl.ds(0, wowners)], send_sems.at[5]).wait()

    all_bytes(upper_ref.at[all_rows], send_sems.at[7]).wait()
    ring_sent()


def exchange(hess_inv, weights, removed):
    rows, cols = lax.axis_size("row"), lax.axis_size("col")
    tall, wide = hess_inv.shape
    count = removed.shape[0]
    share = count // rows
    zs = cols // 2
    vmem = pl.BlockSpec(memory_space=pltpu.VMEM)
    f32, bf16 = jnp.float32, jnp.bfloat16
    dma = pltpu.SemaphoreType.DMA
    return pl.pallas_call(
        functools.partial(exchange_kernel, rows, cols),
        out_shape=(
            jax.ShapeDtypeStruct((count, wide), f32),
            jax.ShapeDtypeStruct((tall, count), f32),
            jax.ShapeDtypeStruct((weights.shape[0], count), bf16),
        ),
        in_specs=[pl.BlockSpec(memory_space=pl.ANY)] * 2 + [vmem],
        out_specs=(vmem,) * 3,
        scratch_shapes=[
            pltpu.VMEM((tall, wide), f32),
            pltpu.VMEM(weights.shape, bf16),
            pltpu.VMEM((count, LANES), jnp.int32),
            dma((2,)),
            pltpu.VMEM((count, count), f32),
            pltpu.VMEM((wide, count), f32),
            pltpu.VMEM((LANES, count), f32),
            pltpu.VMEM((wide, LANES), f32),
            pltpu.VMEM((LANES, LANES), f32),
            pltpu.VMEM((tall // 2, LANES), f32),
            pltpu.VMEM((weights.shape[0], LANES), bf16),
            pltpu.VMEM((rows, share, LANES), f32),
            pltpu.VMEM((rows, share, LANES), f32),
            pltpu.VMEM((share, 1, LANES), f32),
            pltpu.VMEM((cols, 1, LANES), f32),
            pltpu.VMEM((1, count), f32),
            pltpu.VMEM((cols, 1, count), f32),
            pltpu.VMEM((cols, share // 2, LANES), f32),
            pltpu.VMEM((cols, 16, LANES), bf16),
            dma((8,)),
            dma((8,)),
            dma((2 * zs,)),
            dma((2 * zs,)),
            dma((2 * zs,)),
            dma((2 * zs,)),
        ],
        compiler_params=pltpu.CompilerParams(
            collective_id=0, has_side_effects=True, vmem_limit_bytes=60 * 1024 * 1024
        ),
        cost_estimate=pl.CostEstimate(
            flops=2 * tall * wide * LANES * 6, bytes_accessed=8 * 1024 * 1024, transcendentals=0
        ),
        name="exchange",
    )(hess_inv, weights, removed.reshape(count // LANES, LANES))


def update_kernel(
    hess_ref, weight_ref, left_ref, wleft_ref, coupling_ref, hess_out_ref, weight_out_ref, terms_ref
):
    count = coupling_ref.shape[0]

    @pl.when(pl.program_id(0) == 0)
    def _():
        high, mid, _ = split3(coupling_ref[...])
        terms_ref[0:count] = high
        terms_ref[count : 2 * count] = mid
        terms_ref[2 * count : 3 * count] = high

    high, mid, _ = split3(left_ref[...])
    hess_out_ref[...] = hess_ref[...] - jnp.dot(
        jnp.concatenate([mid, high, high], axis=1),
        terms_ref[...],
        preferred_element_type=jnp.float32,
    )
    own = wleft_ref[...]
    change = jnp.dot(
        jnp.concatenate([own, own], axis=1),
        terms_ref[count : 3 * count],
        preferred_element_type=jnp.float32,
    )
    weight_out_ref[...] = (weight_ref[...].astype(jnp.float32) - change).astype(jnp.bfloat16)


def update(hess_inv, weights, left, weight_left, coupling):
    steps = 4
    count, wide = coupling.shape
    tall, high = hess_inv.shape[0] // steps, weights.shape[0] // steps

    def rows_of(size, width):
        return pl.BlockSpec((size, width), lambda i: (i, 0))

    return pl.pallas_call(
        update_kernel,
        grid=(steps,),
        out_shape=(
            jax.ShapeDtypeStruct(hess_inv.shape, jnp.float32),
            jax.ShapeDtypeStruct(weights.shape, jnp.bfloat16),
        ),
        in_specs=[
            rows_of(tall, wide),
            rows_of(high, wide),
            rows_of(tall, count),
            rows_of(high, count),
            pl.BlockSpec((count, wide), lambda i: (0, 0)),
        ],
        out_specs=(rows_of(tall, wide), rows_of(high, wide)),
        scratch_shapes=[pltpu.VMEM((3 * count, wide), jnp.bfloat16)],
        compiler_params=pltpu.CompilerParams(vmem_limit_bytes=60 * 1024 * 1024),
        name="update",
    )(hess_inv, weights, left, weight_left, coupling)


def on_device(hess_inv, weights, removed):
    coupling, left, weight_left = exchange(hess_inv, weights, removed)
    return update(hess_inv, weights, left, weight_left, coupling)


def solution(mesh):
    placed = (P("row", "col"), P("row", "col"), P())
    return jax.shard_map(
        on_device,
        mesh=mesh,
        in_specs=placed,
        out_specs=(P("row", "col"), P("row", "col")),
        check_vma=False,
    )
```
